32 devices in a mesh: dp: 8 (over z, x), tensor: 4 (over y, core).
Axes of the slice: x: 2, y: 2, z: 4, core: 2. Of those that a mesh axis runs over, the one named last changes fastest.
Arguments:
- tokens: bfloat16 [8192, 768], P('dp'), may hold values from -6 to 6
- segment_ids: int32 [8, 1024], P('dp'), may hold values from 0 to 3, as said below
- cotangent: bfloat16 [8192, 768], P('dp'), may hold values from -6 to 6
- first_norm_scale: float32 [768], replicated, may hold values from 0.5 to 1.5
- first_norm_bias: float32 [768], replicated, may hold values from -2 to 2
- qkv_weight: bfloat16 [768, 3, 768], P(None, None, 'tensor'), may hold values from -0.21875 to 0.21875
- qkv_bias: float32 [3, 768], P(None, 'tensor'), may hold values from -2 to 2
- out_weight: bfloat16 [768, 768], P('tensor'), may hold values from -0.875 to 0.875
- out_bias: float32 [768], replicated, may hold values from -2 to 2
- second_norm_scale: float32 [768], replicated, may hold values from 0.5 to 1.5
- second_norm_bias: float32 [768], replicated, may hold values from -2 to 2
- fc_weight: bfloat16 [768, 3072], P(None, 'tensor'), may hold values from -0.21875 to 0.21875
- fc_bias: float32 [3072], P('tensor'), may hold values from -2 to 2
- proj_weight: bfloat16 [3072, 768], P('tensor'), may hold values from -0.109375 to 0.109375
- proj_bias: float32 [768], replicated, may hold values from -2 to 2
Outputs:
- block_out: bfloat16 [8192, 768], P('dp')
- tokens_grad: bfloat16 [8192, 768], P('dp')
- norm1_gain_grad: float32 [768], replicated
- norm1_bias_grad: float32 [768], replicated
- qkv_weight_grad: float32 [768, 3, 768], P('dp', None, 'tensor')
- qkv_bias_grad: float32 [3, 768], P(None, 'tensor')
- out_weight_grad: float32 [768, 768], P('tensor', 'dp')
- out_bias_grad: float32 [768], replicated
- norm2_gain_grad: float32 [768], replicated
- norm2_bias_grad: float32 [768], replicated
- fc_weight_grad: float32 [768, 3072], P('dp', 'tensor')
- fc_bias_grad: float32 [3072], P('tensor')
- proj_weight_grad: float32 [3072, 768], P('tensor', 'dp')
- proj_bias_grad: float32 [768], replicated
The draws below stay inside these ranges and needn't reach their ends.
Inputs may be any that keep to these rules, and one draw needn't show every extreme that they name: `segment_ids`: along each sequence segment numbers start at 0 and rise by one from document to document; every document (a run of equal numbers) holds 60 to 800 neighbouring positions, and each sequence has one document of exactly 800 positions.
All inputs are finite; a program needn't handle non-finite values.
Results may differ from the reference program's by a relative error of at most 0.012.
Values may be sent and summed in bfloat16 or wider, within the bound.
A program may use at most 128 MiB of HBM per device.

```python
import jax
import jax.numpy as jnp
from jax import lax

D = 768
HEADS = 12
FF = 3072
HEAD_DIM = 64
SEQ = 1024
DOC_MOST = 800
DOC_LEAST = 60
SEQUENCES = 8
TOKENS = 8192


def draw_segment_ids(key, part):
    key = jax.random.fold_in(key, 11)
    remaining = SEQ - DOC_MOST
    most_pieces = remaining // DOC_LEAST
    slots = jnp.arange(most_pieces, dtype=jnp.int32)
    spots = jnp.arange(most_pieces + 1, dtype=jnp.int32)
    places = jnp.arange(SEQ, dtype=jnp.int32)

    def one_sequence(seq_key, forced):
        count_key, cut_key, place_key = jax.random.split(seq_key, 3)
        drawn = jax.random.randint(count_key, (), 1, most_pieces + 1).astype(jnp.int32)
        count = jnp.where(forced, jnp.int32(most_pieces), drawn)
        spare = (remaining - count * DOC_LEAST).astype(jnp.int32)
        cuts = jax.random.randint(cut_key, (most_pieces,), 0, spare + 1).astype(jnp.int32)
        cuts = jnp.where(slots < count - 1, cuts, spare)
        cuts = jnp.sort(cuts)
        lower = jnp.concatenate([jnp.zeros((1,), jnp.int32), cuts[:-1]])
        pieces = jnp.where(slots < count, DOC_LEAST + cuts - lower, 0).astype(jnp.int32)
        place = jax.random.randint(place_key, (), 0, count + 1).astype(jnp.int32)
        padded = jnp.concatenate([pieces, jnp.zeros((1,), jnp.int32)])
        shifted = jnp.concatenate([jnp.zeros((1,), jnp.int32), pieces])
        lengths = jnp.where(spots < place, padded, jnp.where(spots == place, jnp.int32(DOC_MOST), shifted))
        ends = jnp.cumsum(lengths).astype(jnp.int32)
        return jnp.sum((places[:, None] >= ends[None, :]).astype(jnp.int32), axis=1).astype(jnp.int32)
    seq_keys = jax.random.split(key, SEQUENCES)
    forced = jnp.arange(SEQUENCES) == 0
    return jax.vmap(one_sequence)(seq_keys, forced).astype(jnp.int32)


def level_of(own_key, extent, shards, low, top_value):
    gain = 1.0
    for axis_at, blocks in shards:
        heights = jax.random.uniform(jax.random.fold_in(jax.random.fold_in(own_key, 6), axis_at), (blocks,), jnp.float32, low / len(shards), top_value / len(shards))
        gain = gain * jnp.repeat(jnp.exp(heights), extent[axis_at] // blocks).reshape((-1,) + (1,) * (len(extent) - 1 - axis_at))
    return gain


def noise(rng, dims, width, reach, cuts=(), kind=jnp.bfloat16):
    entries = width * jax.random.normal(rng, dims, jnp.float32)
    if cuts:
        entries = entries * level_of(rng, dims, cuts, -0.22, 0.18)
    return jnp.clip(entries, -reach, reach).astype(kind)


def setup_inputs(seed: int = 0) -> dict:
    streams_of = jax.random.split(jax.random.key(seed), 16)
    return {
        "tokens": noise(streams_of[0], (TOKENS, D), 1.0, 6.0, ((0, 8),)),
        "segment_ids": draw_segment_ids(jax.random.fold_in(streams_of[15], 71), 0),
        "cotangent": noise(streams_of[2], (TOKENS, D), 1.0, 6.0, ((0, 8),)),
        "first_norm_scale": jnp.clip(1.0 + 0.1 * jax.random.normal(streams_of[3], (D,), jnp.float32), 0.5, 1.5),
        "first_norm_bias": noise(streams_of[4], (D,), 0.3, 2.0, (), jnp.float32),
        "qkv_weight": noise(streams_of[5], (D, 3, D), D ** -0.5, 0.21875, ((2, 4),)),
        "qkv_bias": noise(streams_of[6], (3, D), 0.3, 2.0, ((1, 4),), jnp.float32),
        "out_weight": noise(streams_of[7], (D, D), (D // 16) ** -0.5, 0.875, ((0, 4),)),
        "out_bias": noise(streams_of[8], (D,), 0.3, 2.0, (), jnp.float32),
        "second_norm_scale": jnp.clip(1.0 + 0.1 * jax.random.normal(streams_of[9], (D,), jnp.float32), 0.5, 1.5),
        "second_norm_bias": noise(streams_of[10], (D,), 0.3, 2.0, (), jnp.float32),
        "fc_weight": noise(streams_of[11], (D, FF), D ** -0.5, 0.21875, ((1, 4),)),
        "fc_bias": noise(streams_of[12], (FF,), 0.3, 2.0, ((0, 4),), jnp.float32),
        "proj_weight": noise(streams_of[13], (FF, D), FF ** -0.5, 0.109375, ((0, 4),)),
        "proj_bias": noise(streams_of[14], (D,), 0.3, 2.0, (), jnp.float32),
    }


@jax.custom_vjp
def low(v):
    return lax.optimization_barrier(v.astype(jnp.bfloat16)).astype(jnp.float32)

@jax.custom_vjp
def low_back(v):
    return v

def low_keep(v):
    return (low(v), None)

def low_pass(kept, grad):
    return (grad,)

def back_keep(v):
    return (v, None)

def back_low(kept, grad):
    return (low(grad),)
low.defvjp(low_keep, low_pass)
low_back.defvjp(back_keep, back_low)
exact = lax.Precision.HIGHEST

def layer_norm(row_values, norm_gain, norm_shift):
    row_mean = lax.optimization_barrier(jnp.mean(row_values, axis=-1, keepdims=True))
    centered = row_values - row_mean
    variance = lax.optimization_barrier(jnp.mean(centered * centered, axis=-1, keepdims=True))
    return centered * lax.rsqrt(variance + 1e-05) * norm_gain + norm_shift

def gelu_tanh(values_in):
    return 0.5 * values_in * (1.0 + jnp.tanh(0.7978845608 * (values_in + 0.044715 * values_in * values_in * values_in)))

def forward_sequence(params, row_values, segment):
    gain_one, shift_one, qkv_w, qkv_b, out_w, out_b, gain_two, shift_two, fc_w, fc_b, proj_w, proj_b = params
    first_normed_input = low(layer_norm(row_values, gain_one, shift_one))
    projected = jnp.einsum('td,dcf->ctf', first_normed_input, qkv_w, precision=exact) + qkv_b[:, None, :]
    projected = low(low_back(projected))
    split_heads = projected.reshape(3, SEQ, HEADS, HEAD_DIM)
    queries, key_rows, values = (split_heads[0], split_heads[1], split_heads[2])
    scores = jnp.einsum('qhe,khe->hqk', queries, key_rows, precision=exact) * HEAD_DIM ** (-0.5)
    scores = low_back(scores)
    position = jnp.arange(SEQ)
    allowed = (segment[:, None] == segment[None, :]) & (position[None, :] <= position[:, None])
    scores = jnp.where(allowed[None], scores, -1000000000.0)
    row_probs = jax.nn.softmax(scores, axis=-1)
    mixed_rows = jnp.einsum('hqk,khe->qhe', low(row_probs), values, precision=exact).reshape(SEQ, D)
    mixed_rows = low(low_back(mixed_rows))
    attn_out = low_back(jnp.dot(mixed_rows, out_w, precision=exact) + out_b)
    midway_state = row_values + attn_out
    second_normed_input = low(layer_norm(midway_state, gain_two, shift_two))
    hidden_pre = low_back(jnp.dot(second_normed_input, fc_w, precision=exact) + fc_b)
    hidden_act = low(gelu_tanh(hidden_pre))
    mlp_out = low_back(jnp.dot(hidden_act, proj_w, precision=exact) + proj_b)
    return midway_state + mlp_out

def reference(tokens, segment_ids, cotangent, first_norm_scale, first_norm_bias, qkv_weight, qkv_bias, out_weight, out_bias, second_norm_scale, second_norm_bias, fc_weight, fc_bias, proj_weight, proj_bias):
    params = tuple((item.astype(jnp.float32) for item in (first_norm_scale, first_norm_bias, qkv_weight, qkv_bias, out_weight, out_bias, second_norm_scale, second_norm_bias, fc_weight, fc_bias, proj_weight, proj_bias)))
    seq_tokens = tokens.astype(jnp.float32).reshape(-1, SEQ, D)
    seq_cot = cotangent.astype(jnp.float32).reshape(-1, SEQ, D)

    def one_sequence(carried, seq_item):
        row_values, segment, cot_rows = seq_item

        def run(param_set, inputs_now):
            return forward_sequence(param_set, inputs_now, segment)
        result, pullback = jax.vjp(run, params, row_values)
        param_grads, input_gradient = pullback(cot_rows)
        carried = jax.tree.map(jnp.add, carried, param_grads)
        return (carried, (result.astype(jnp.bfloat16), input_gradient.astype(jnp.bfloat16)))
    zero_grads = jax.tree.map(jnp.zeros_like, params)
    grad_sums, (outputs_seq, grads_seq) = lax.scan(one_sequence, zero_grads, (seq_tokens, segment_ids, seq_cot))
    return (outputs_seq.reshape(-1, D), grads_seq.reshape(-1, D), grad_sums[0], grad_sums[1], grad_sums[2], grad_sums[3], grad_sums[4], grad_sums[5], grad_sums[6], grad_sums[7], grad_sums[8], grad_sums[9], grad_sums[10], grad_sums[11])
```

```python
import functools

import jax
import jax.numpy as jnp
from jax import lax
from jax.experimental import pallas as pl
from jax.experimental.pallas import tpu as pltpu
from jax.sharding import PartitionSpec as P

HEADS = 12
MESH = pl.DeviceIdType.MESH
VMEM = pl.BlockSpec(memory_space=pltpu.VMEM)
CHUNKS = 4


def layer_statistics(row_values):
    row_mean = jnp.mean(row_values, axis=-1, keepdims=True)
    centered = row_values - row_mean
    inverse = lax.rsqrt(jnp.mean(centered * centered, axis=-1, keepdims=True) + 1e-05)
    return (centered * inverse, inverse)


def norm_backward_pass(normed_grad, normalized, inverse, norm_gain):
    scaled = normed_grad * norm_gain
    return inverse * (
        scaled
        - jnp.mean(scaled, axis=-1, keepdims=True)
        - normalized * jnp.mean(scaled * normalized, axis=-1, keepdims=True)
    )


def gelu_tanh(values_in):
    return (
        0.5
        * values_in
        * (
            1.0
            + jnp.tanh(0.7978845608 * (values_in + 0.044715 * values_in * values_in * values_in))
        )
    )


def inner_rows(left_rows, right_rows):
    return lax.dot_general(
        left_rows, right_rows, (((0,), (0,)), ((), ())), preferred_element_type=jnp.float32
    )


def times_transposed(left_rows, right_rows):
    return lax.dot_general(
        left_rows, right_rows, (((1,), (1,)), ((), ())), preferred_element_type=jnp.float32
    )


def visible(segment, first_row, block_rows):
    last_key = first_row + block_rows
    columns = jnp.arange(last_key)
    rows_at = first_row + jnp.arange(block_rows)
    rows_seg = segment[first_row:last_key]
    return (rows_seg[:, None] == segment[None, :last_key]) & (columns[None, :] <= rows_at[:, None])


def block_scores(rows_q, key_rows, segment, first_row, block_rows):
    score_scale = rows_q.shape[-1] ** (-0.5)
    scores = (
        jnp.einsum("qhe,khe->hqk", rows_q, key_rows, preferred_element_type=jnp.float32)
        * score_scale
    )
    allowed = visible(segment, first_row, block_rows)
    return (jnp.where(allowed[None], scores, -1000000000.0), allowed)


def attend_sequence(seq_item):
    queries, key_rows, values, segment = seq_item
    seq_length = segment.shape[0]
    block_rows = min(512, seq_length)
    mixed_parts = []
    logsum_parts = []
    for block_index in range(seq_length // block_rows):
        first_row = block_index * block_rows
        last_key = first_row + block_rows
        rows_q = queries[first_row:last_key]
        scores, allowed = block_scores(rows_q, key_rows[:last_key], segment, first_row, block_rows)
        row_max = jnp.max(scores, axis=-1, keepdims=True)
        weights = jnp.exp(scores - row_max)
        row_total = jnp.sum(weights, axis=-1, keepdims=True)
        row_probs = (weights / row_total).astype(jnp.bfloat16)
        mixed_parts.append(
            jnp.einsum(
                "hqk,khe->qhe", row_probs, values[:last_key], preferred_element_type=jnp.float32
            )
        )
        logsum_parts.append(row_max + jnp.log(row_total))
    return (jnp.concatenate(mixed_parts, axis=0), jnp.stack(logsum_parts))


def attend_back(seq_item):
    queries, key_rows, values, grad_heads, logsum, segment = seq_item
    seq_length = segment.shape[0]
    block_rows = min(512, seq_length)
    score_scale = queries.shape[-1] ** (-0.5)
    key_grad = jnp.zeros(key_rows.shape, jnp.float32)
    value_grad = jnp.zeros(key_rows.shape, jnp.float32)
    query_parts = []
    for block_index in range(seq_length // block_rows):
        first_row = block_index * block_rows
        last_key = first_row + block_rows
        rows_q = queries[first_row:last_key]
        rows_g = grad_heads[first_row:last_key]
        seen_keys = key_rows[:last_key]
        seen_values = values[:last_key]
        scores, allowed = block_scores(rows_q, seen_keys, segment, first_row, block_rows)
        row_probs = jnp.where(allowed[None], jnp.exp(scores - logsum[block_index]), 0.0)
        value_grad = value_grad.at[:last_key].add(
            jnp.einsum(
                "hqk,qhe->khe",
                row_probs.astype(jnp.bfloat16),
                rows_g,
                preferred_element_type=jnp.float32,
            )
        )
        prob_grad = jnp.einsum(
            "qhe,khe->hqk", rows_g, seen_values, preferred_element_type=jnp.float32
        )
        centre = jnp.sum(row_probs * prob_grad, axis=-1, keepdims=True)
        score_grad = (row_probs * (prob_grad - centre)).astype(jnp.bfloat16)
        query_parts.append(
            jnp.einsum("hqk,khe->qhe", score_grad, seen_keys, preferred_element_type=jnp.float32)
            * score_scale
        )
        key_grad = key_grad.at[:last_key].add(
            jnp.einsum("hqk,qhe->khe", score_grad, rows_q, preferred_element_type=jnp.float32)
            * score_scale
        )
    return (jnp.concatenate(query_parts, axis=0), key_grad, value_grad)


def greet(peers):
    barrier = pltpu.get_barrier_semaphore()
    for peer in peers:
        pl.semaphore_signal(barrier, inc=1, device_id=peer, device_id_type=MESH)
    pl.semaphore_wait(barrier, len(peers))


def send(src, dst, send_sem, recv_sem, peer):
    return pltpu.make_async_remote_copy(
        src_ref=src,
        dst_ref=dst,
        send_sem=send_sem,
        recv_sem=recv_sem,
        device_id=peer,
        device_id_type=MESH,
    )


def tensor_peers():
    me = lax.axis_index("tensor")
    core = lax.rem(me, 2)
    mate = me + 1 - 2 * core
    across = lax.rem(me + 2, 4)
    return me, core, mate, across


def mix_kernel(mixed_ref, weight_ref, out_ref, held, s_mate, r_mate, s_far, r_far, s_fwd, r_fwd):
    me, core, mate, across = tensor_peers()
    mate_id, far_id = {"tensor": mate}, {"tensor": across}
    greet([mate_id, far_id])
    chunks = mixed_ref.shape[0]
    far, near, fwd = [], [], []
    for j in range(chunks):
        copy = send(mixed_ref.at[j], held.at[1, j], s_far.at[j], r_far.at[j], far_id)
        copy.start()
        far.append(copy)
    for j in range(chunks):
        copy = send(mixed_ref.at[j], held.at[0, j], s_mate.at[j], r_mate.at[j], mate_id)
        copy.start()
        near.append(copy)
    for j in range(chunks):
        far[j].wait_recv()
        copy = send(held.at[1, j], held.at[2, j], s_fwd.at[j], r_fwd.at[j], mate_id)
        copy.start()
        fwd.append(copy)
    for j in range(chunks):
        near[j].wait_recv()
        fwd[j].wait_recv()
        own = mixed_ref[j]
        near_rows = held[0, j]
        far_rows = held[1, j]
        fwd_rows = held[2, j]
        low_near = jnp.where(core == 0, own, near_rows)
        high_near = jnp.where(core == 0, near_rows, own)
        low_far = jnp.where(core == 0, far_rows, fwd_rows)
        high_far = jnp.where(core == 0, fwd_rows, far_rows)
        upper = me >= 2
        rows = [
            jnp.where(upper, low_far, low_near),
            jnp.where(upper, high_far, high_near),
            jnp.where(upper, low_near, low_far),
            jnp.where(upper, high_near, high_far),
        ]
        total = jnp.zeros(out_ref.shape[1:], jnp.float32)
        for g in range(4):
            total = total + jnp.dot(rows[g], weight_ref[g], preferred_element_type=jnp.float32)
        out_ref[j] = total
    for j in range(chunks):
        far[j].wait_send()
        near[j].wait_send()
        fwd[j].wait_send()


def mix_out(mixed_low, weight_full):
    rows, local_width = mixed_low.shape
    width = weight_full.shape[-1]
    blocks = mixed_low.reshape(CHUNKS, rows // CHUNKS, local_width)
    out = pl.pallas_call(
        mix_kernel,
        out_shape=jax.ShapeDtypeStruct((CHUNKS, rows // CHUNKS, width), jnp.float32),
        in_specs=[VMEM] * 2,
        out_specs=VMEM,
        scratch_shapes=[pltpu.VMEM((3,) + blocks.shape, jnp.bfloat16)]
        + [pltpu.SemaphoreType.DMA((CHUNKS,))] * 6,
        compiler_params=pltpu.CompilerParams(
            collective_id=0, has_side_effects=True, vmem_limit_bytes=48 * 1024 * 1024
        ),
    )(blocks, weight_full)
    return out.reshape(rows, width)


def exchange_kernel(n_sum, n_grad, has_small, dp, *refs):
    refs = list(refs)

    def take(count):
        taken = refs[:count]
        del refs[:count]
        return taken

    sums = take(n_sum)
    grads = take(n_grad)
    small = take(1)[0] if has_small else None
    sum_outs = take(n_sum)
    grad_outs = take(n_grad)
    small_out = take(1)[0] if has_small else None
    from_mate = take(n_sum)
    chip_sum = take(n_sum)
    from_far = take(n_sum)
    pair_in = take(n_grad)
    pair_sum = take(n_grad)
    line_in = take(n_grad)
    small_in = take(1)[0] if has_small else None
    s1, r1, s2, r2, s3, r3, sx, rx, sz, rz = take(10)
    ss, rs = take(2) if has_small else (None, None)

    me, core, mate, across = tensor_peers()
    mate_id, far_id = {"tensor": mate}, {"tensor": across}
    here = lax.axis_index("dp")
    side = lax.rem(here, 2)
    line = here // 2
    length = dp // 2
    pair_id = {"dp": here + 1 - 2 * side}
    places = [lax.rem(line + k, length) for k in range(length)]
    line_ids = [{"dp": places[k] * 2 + side} for k in range(length)]
    all_ids = [{"dp": lax.rem(here + k, dp)} for k in range(dp)]
    if has_small:
        greet([mate_id, far_id] + all_ids[1:])
    else:
        greet([mate_id, far_id, pair_id] + line_ids[1:])

    started = []
    chunks = CHUNKS
    first = [[None] * chunks for _ in range(n_sum)]
    second = [[None] * chunks for _ in range(n_sum)]
    third = [[None] * chunks for _ in range(n_sum)]
    for i in range(n_sum):
        for j in range(chunks):
            first[i][j] = send(
                sums[i].at[1 - core, j], from_mate[i].at[j], s1.at[i, j], r1.at[i, j], mate_id
            )
            first[i][j].start()
    order = list(range(1, length)) + [0]
    pair = [[None] * length for _ in range(n_grad)]
    for k in order:
        for g in range(n_grad):
            pair[g][k] = send(
                grads[g].at[places[k], 1 - side],
                pair_in[g].at[k],
                sx.at[g, k],
                rx.at[g, k],
                pair_id,
            )
            pair[g][k].start()
    little = []
    if has_small:
        for k in range(1, dp):
            copy = send(small, small_in.at[dp - k], ss.at[k], rs.at[dp - k], all_ids[k])
            copy.start()
            little.append(copy)

    for i in range(n_sum):
        for j in range(chunks):
            first[i][j].wait_recv()
            chip_sum[i][j] = (
                sums[i][core, j].astype(jnp.float32) + from_mate[i][j].astype(jnp.float32)
            ).astype(jnp.bfloat16)
            second[i][j] = send(
                chip_sum[i].at[j], from_far[i].at[j], s2.at[i, j], r2.at[i, j], far_id
            )
            second[i][j].start()

    across_line = [[None] * length for _ in range(n_grad)]
    for k in order:
        for g in range(n_grad):
            pair[g][k].wait_recv()
            pair_sum[g][k] = (
                grads[g][places[k], side].astype(jnp.float32) + pair_in[g][k].astype(jnp.float32)
            ).astype(jnp.bfloat16)
            if k:
                across_line[g][k] = send(
                    pair_sum[g].at[k],
                    line_in[g].at[length - k],
                    sz.at[g, k],
                    rz.at[g, length - k],
                    line_ids[k],
                )
                across_line[g][k].start()

    for i in range(n_sum):
        for j in range(chunks):
            second[i][j].wait_recv()
            sum_outs[i][core, j] = (
                chip_sum[i][j].astype(jnp.float32) + from_far[i][j].astype(jnp.float32)
            ).astype(jnp.bfloat16)
            third[i][j] = send(
                sum_outs[i].at[core, j],
                sum_outs[i].at[core, j],
                s3.at[i, j],
                r3.at[i, j],
                mate_id,
            )
            third[i][j].start()

    for g in range(n_grad):
        total = pair_sum[g][0].astype(jnp.float32)
        for k in range(1, length):
            across_line[g][length - k].wait_recv()
            total = total + line_in[g][k].astype(jnp.float32)
        grad_outs[g][...] = total
    if has_small:
        for copy in little:
            copy.wait_recv()
        small_in[0] = small[...]
        total = small_in[lax.rem(dp - here, dp)]
        for source in range(1, dp):
            total = total + small_in[lax.rem(source + dp - here, dp)]
        small_out[...] = total
    for i in range(n_sum):
        for j in range(chunks):
            third[i][j].wait_recv()
            first[i][j].wait_send()
            second[i][j].wait_send()
            third[i][j].wait_send()
    for g in range(n_grad):
        for k in range(length):
            pair[g][k].wait_send()
            if k:
                across_line[g][k].wait_send()
    for copy in little:
        copy.wait_send()


def exchange(sums, grads, small, dp, collective_id):
    rows, width = sums[0].shape
    chunk_rows = rows // (2 * CHUNKS)
    sum_shape = (2, CHUNKS, chunk_rows, width)
    half_shape = sum_shape[1:]
    sums = [item.astype(jnp.bfloat16).reshape(sum_shape) for item in sums]
    length = dp // 2
    shares = [(item.shape[0] // dp, item.shape[1]) for item in grads]
    grads = [
        item.astype(jnp.bfloat16).reshape((length, 2) + share)
        for item, share in zip(grads, shares)
    ]
    n_sum, n_grad = len(sums), len(grads)
    has_small = small is not None
    operands = sums + grads + ([small] if has_small else [])
    out_shape = [jax.ShapeDtypeStruct(sum_shape, jnp.bfloat16)] * n_sum
    out_shape += [jax.ShapeDtypeStruct(share, jnp.float32) for share in shares]
    if has_small:
        out_shape.append(jax.ShapeDtypeStruct(small.shape, small.dtype))
    scratch = [pltpu.VMEM(half_shape, jnp.bfloat16)] * (3 * n_sum)
    for _ in range(3):
        scratch += [pltpu.VMEM((length,) + share, jnp.bfloat16) for share in shares]
    if has_small:
        scratch.append(pltpu.VMEM((dp,) + small.shape, jnp.float32))
    scratch += [pltpu.SemaphoreType.DMA((n_sum, CHUNKS))] * 6
    scratch += [pltpu.SemaphoreType.DMA((n_grad, length))] * 4
    if has_small:
        scratch += [pltpu.SemaphoreType.DMA((dp,))] * 2
    outs = pl.pallas_call(
        functools.partial(exchange_kernel, n_sum, n_grad, has_small, dp),
        out_shape=out_shape,
        in_specs=[VMEM] * len(operands),
        out_specs=[VMEM] * len(out_shape),
        scratch_shapes=scratch,
        compiler_params=pltpu.CompilerParams(
            collective_id=collective_id,
            has_side_effects=True,
            vmem_limit_bytes=48 * 1024 * 1024,
        ),
    )(*operands)
    summed = [item.reshape(rows, width) for item in outs[:n_sum]]
    scattered = list(outs[n_sum : n_sum + n_grad])
    return summed, scattered, (outs[-1] if has_small else None)


def local(
    tokens,
    segment_ids,
    cotangent,
    first_norm_scale,
    first_norm_bias,
    qkv_weight,
    qkv_bias,
    out_weight,
    out_bias,
    second_norm_scale,
    second_norm_bias,
    fc_weight,
    fc_bias,
    proj_weight,
    proj_bias,
):
    total_rows, model_width = tokens.shape
    dp = lax.axis_size("dp")
    seq_count, seq_length = segment_ids.shape
    local_width = out_weight.shape[0]
    head_dim = model_width // HEADS
    local_heads = local_width // head_dim

    out_weight_full = lax.all_gather(out_weight, "tensor", axis=0)
    residual = tokens.astype(jnp.float32)
    xhat_one, rstd_one = layer_statistics(residual)
    normed_one = (xhat_one * first_norm_scale + first_norm_bias).astype(jnp.bfloat16)
    qkv_low = [
        (
            jnp.dot(normed_one, qkv_weight[:, c], preferred_element_type=jnp.float32)
            + qkv_bias[c]
        )
        .astype(jnp.bfloat16)
        .reshape(seq_count, seq_length, local_heads, head_dim)
        for c in range(3)
    ]
    forward = [
        attend_sequence((qkv_low[0][i], qkv_low[1][i], qkv_low[2][i], segment_ids[i]))
        for i in range(seq_count)
    ]
    mixed_low = (
        jnp.stack([item[0] for item in forward])
        .reshape(total_rows, local_width)
        .astype(jnp.bfloat16)
    )
    middle = residual + mix_out(mixed_low, out_weight_full) + out_bias
    xhat_two, rstd_two = layer_statistics(middle)
    normed_two = (xhat_two * second_norm_scale + second_norm_bias).astype(jnp.bfloat16)
    hidden_pre = jnp.dot(normed_two, fc_weight, preferred_element_type=jnp.float32) + fc_bias
    hidden_act, gelu_pull = jax.vjp(gelu_tanh, hidden_pre)
    hidden_low = hidden_act.astype(jnp.bfloat16)
    out_part = jnp.dot(hidden_low, proj_weight, preferred_element_type=jnp.float32)
    cot = cotangent.astype(jnp.float32)
    proj_bias_grad = jnp.sum(cot, axis=0)
    proj_grad = inner_rows(cotangent, hidden_low)
    act_grad = times_transposed(cotangent, proj_weight)
    pre_grad = gelu_pull(act_grad)[0].astype(jnp.bfloat16)
    fc_bias_grad = jnp.sum(pre_grad.astype(jnp.float32), axis=0)
    fc_grad = inner_rows(normed_two, pre_grad)
    normed_two_part = times_transposed(pre_grad, fc_weight)

    (normed_two_grad, branch), (proj_sum, fc_sum), _ = exchange(
        [normed_two_part, out_part], [proj_grad, fc_grad], None, dp, 1
    )
    block_out = (middle + branch.astype(jnp.float32) + proj_bias).astype(jnp.bfloat16)
    normed_two_grad = normed_two_grad.astype(jnp.float32)
    gain_two_grad = jnp.sum(normed_two_grad * xhat_two, axis=0)
    shift_two_grad = jnp.sum(normed_two_grad, axis=0)
    middle_grad = cot + norm_backward_pass(normed_two_grad, xhat_two, rstd_two, second_norm_scale)
    middle_low = middle_grad.astype(jnp.bfloat16)
    out_bias_grad = jnp.sum(middle_low.astype(jnp.float32), axis=0)
    out_grad = inner_rows(middle_low, mixed_low)
    grad_heads = (
        times_transposed(middle_low, out_weight)
        .astype(jnp.bfloat16)
        .reshape(seq_count, seq_length, local_heads, head_dim)
    )
    backward = [
        attend_back(
            (
                qkv_low[0][i],
                qkv_low[1][i],
                qkv_low[2][i],
                grad_heads[i],
                forward[i][1],
                segment_ids[i],
            )
        )
        for i in range(seq_count)
    ]
    qkv_grad = jnp.concatenate(
        [
            jnp.stack([item[c] for item in backward])
            .reshape(total_rows, local_width)
            .astype(jnp.bfloat16)
            for c in range(3)
        ],
        axis=1,
    )
    qkv_bias_grad = jnp.sum(qkv_grad.astype(jnp.float32), axis=0)
    qkv_weight_grad = inner_rows(normed_one, qkv_grad)
    normed_one_part = times_transposed(
        qkv_grad, qkv_weight.reshape(model_width, 3 * local_width)
    )
    small_parts = [
        gain_two_grad,
        shift_two_grad,
        out_bias_grad,
        proj_bias_grad,
        fc_bias_grad,
        qkv_bias_grad,
    ]
    small = jnp.concatenate(small_parts)
    small = jnp.pad(small, (0, -small.shape[0] % 1024)).reshape(-1, 128)
    (normed_one_grad,), (qkv_sum, out_sum), small_sum = exchange(
        [normed_one_part], [qkv_weight_grad, out_grad], small, dp, 2
    )
    normed_one_grad = normed_one_grad.astype(jnp.float32)
    gain_one_grad, shift_one_grad = lax.psum(
        (jnp.sum(normed_one_grad * xhat_one, axis=0), jnp.sum(normed_one_grad, axis=0)), "dp"
    )
    tokens_grad = middle_grad + norm_backward_pass(
        normed_one_grad, xhat_one, rstd_one, first_norm_scale
    )
    flat = small_sum.reshape(-1)
    summed = []
    at = 0
    for part in small_parts:
        summed.append(flat[at : at + part.shape[0]])
        at += part.shape[0]
    share = model_width // dp
    return (
        block_out,
        tokens_grad.astype(jnp.bfloat16),
        gain_one_grad,
        shift_one_grad,
        qkv_sum.reshape(share, 3, local_width),
        summed[5].reshape(3, local_width),
        out_sum.T,
        summed[2],
        summed[0],
        summed[1],
        fc_sum,
        summed[4],
        proj_sum.T,
        summed[3],
    )


def solution(mesh):
    in_specs = (
        P("dp", None),
        P("dp", None),
        P("dp", None),
        P(),
        P(),
        P(None, None, "tensor"),
        P(None, "tensor"),
        P("tensor", None),
        P(),
        P(),
        P(),
        P(None, "tensor"),
        P("tensor"),
        P("tensor", None),
        P(),
    )
    out_specs = (
        P("dp", None),
        P("dp", None),
        P(),
        P(),
        P("dp", None, "tensor"),
        P(None, "tensor"),
        P("tensor", "dp"),
        P(),
        P(),
        P(),
        P("dp", "tensor"),
        P("tensor"),
        P("tensor", "dp"),
        P(),
    )
    return jax.shard_map(local, mesh=mesh, in_specs=in_specs, out_specs=out_specs, check_vma=False)
```

```python
import functools

import jax
import jax.numpy as jnp
from jax import lax
from jax.experimental import pallas as pl
from jax.experimental.pallas import tpu as pltpu
from jax.sharding import PartitionSpec as P

HEADS = 12
MESH = pl.DeviceIdType.MESH
VMEM = pl.BlockSpec(memory_space=pltpu.VMEM)
CHUNKS = 4
HEAD_ROWS = 2


def layer_statistics(row_values):
    row_mean = jnp.mean(row_values, axis=-1, keepdims=True)
    centered = row_values - row_mean
    inverse = lax.rsqrt(jnp.mean(centered * centered, axis=-1, keepdims=True) + 1e-05)
    return (centered * inverse, inverse)


def norm_backward_pass(normed_grad, normalized, inverse, norm_gain):
    scaled = normed_grad * norm_gain
    return inverse * (
        scaled
        - jnp.mean(scaled, axis=-1, keepdims=True)
        - normalized * jnp.mean(scaled * normalized, axis=-1, keepdims=True)
    )


def gelu_tanh(values_in):
    return (
        0.5
        * values_in
        * (
            1.0
            + jnp.tanh(0.7978845608 * (values_in + 0.044715 * values_in * values_in * values_in))
        )
    )


def inner_rows(left_rows, right_rows):
    return lax.dot_general(
        left_rows, right_rows, (((0,), (0,)), ((), ())), preferred_element_type=jnp.float32
    )


def times_transposed(left_rows, right_rows):
    return lax.dot_general(
        left_rows, right_rows, (((1,), (1,)), ((), ())), preferred_element_type=jnp.float32
    )


def visible(segment, first_row, block_rows):
    last_key = first_row + block_rows
    columns = jnp.arange(last_key)
    rows_at = first_row + jnp.arange(block_rows)
    rows_seg = segment[first_row:last_key]
    return (rows_seg[:, None] == segment[None, :last_key]) & (columns[None, :] <= rows_at[:, None])


def block_scores(rows_q, key_rows, segment, first_row, block_rows):
    score_scale = rows_q.shape[-1] ** (-0.5)
    scores = (
        jnp.einsum("qhe,khe->hqk", rows_q, key_rows, preferred_element_type=jnp.float32)
        * score_scale
    )
    allowed = visible(segment, first_row, block_rows)
    return (jnp.where(allowed[None], scores, -1000000000.0), allowed)


def attend_sequence(seq_item):
    queries, key_rows, values, segment = seq_item
    seq_length = segment.shape[0]
    block_rows = min(512, seq_length)
    mixed_parts = []
    logsum_parts = []
    for block_index in range(seq_length // block_rows):
        first_row = block_index * block_rows
        last_key = first_row + block_rows
        rows_q = queries[first_row:last_key]
        scores, allowed = block_scores(rows_q, key_rows[:last_key], segment, first_row, block_rows)
        row_max = jnp.max(scores, axis=-1, keepdims=True)
        weights = jnp.exp(scores - row_max)
        row_total = jnp.sum(weights, axis=-1, keepdims=True)
        row_probs = (weights / row_total).astype(jnp.bfloat16)
        mixed_parts.append(
            jnp.einsum(
                "hqk,khe->qhe", row_probs, values[:last_key], preferred_element_type=jnp.float32
            )
        )
        logsum_parts.append(row_max + jnp.log(row_total))
    return (jnp.concatenate(mixed_parts, axis=0), jnp.stack(logsum_parts))


def attend_back(seq_item, arriving):
    queries, key_rows, values, grad_heads, logsum, segment = seq_item
    seq_length = segment.shape[0]
    block_rows = min(512, seq_length)
    score_scale = queries.shape[-1] ** (-0.5)
    key_grad = jnp.zeros(key_rows.shape, jnp.float32)
    value_grad = jnp.zeros(key_rows.shape, jnp.float32)
    query_parts = []
    for block_index in range(seq_length // block_rows):
        first_row = block_index * block_rows
        last_key = first_row + block_rows
        rows_q = queries[first_row:last_key]
        rows_g = grad_heads[first_row:last_key]
        if block_index == 1:
            rows_g, arriving, key_grad = lax.optimization_barrier((rows_g, arriving, key_grad))
        seen_keys = key_rows[:last_key]
        seen_values = values[:last_key]
        scores, allowed = block_scores(rows_q, seen_keys, segment, first_row, block_rows)
        row_probs = jnp.where(allowed[None], jnp.exp(scores - logsum[block_index]), 0.0)
        value_grad = value_grad.at[:last_key].add(
            jnp.einsum(
                "hqk,qhe->khe",
                row_probs.astype(jnp.bfloat16),
                rows_g,
                preferred_element_type=jnp.float32,
            )
        )
        prob_grad = jnp.einsum(
            "qhe,khe->hqk", rows_g, seen_values, preferred_element_type=jnp.float32
        )
        centre = jnp.sum(row_probs * prob_grad, axis=-1, keepdims=True)
        score_grad = (row_probs * (prob_grad - centre)).astype(jnp.bfloat16)
        query_parts.append(
            jnp.einsum("hqk,khe->qhe", score_grad, seen_keys, preferred_element_type=jnp.float32)
            * score_scale
        )
        key_grad = key_grad.at[:last_key].add(
            jnp.einsum("hqk,qhe->khe", score_grad, rows_q, preferred_element_type=jnp.float32)
            * score_scale
        )
    return (jnp.concatenate(query_parts, axis=0), key_grad, value_grad), arriving


def greet(peers):
    barrier = pltpu.get_barrier_semaphore()
    for peer in peers:
        pl.semaphore_signal(barrier, inc=1, device_id=peer, device_id_type=MESH)
    pl.semaphore_wait(barrier, len(peers))


def send(src, dst, send_sem, recv_sem, peer):
    return pltpu.make_async_remote_copy(
        src_ref=src,
        dst_ref=dst,
        send_sem=send_sem,
        recv_sem=recv_sem,
        device_id=peer,
        device_id_type=MESH,
    )


def tensor_peers():
    me = lax.axis_index("tensor")
    core = lax.rem(me, 2)
    mate = me + 1 - 2 * core
    across = lax.rem(me + 2, 4)
    return me, core, mate, across


def mix_kernel(mixed_ref, weight_ref, out_ref, held, s_mate, r_mate, s_far, r_far, s_fwd, r_fwd):
    me, core, mate, across = tensor_peers()
    mate_id, far_id = {"tensor": mate}, {"tensor": across}
    greet([mate_id, far_id])
    chunks = mixed_ref.shape[0]
    far, near, fwd = [], [], []
    for j in range(chunks):
        copy = send(mixed_ref.at[j], held.at[1, j], s_far.at[j], r_far.at[j], far_id)
        copy.start()
        far.append(copy)
    for j in range(chunks):
        copy = send(mixed_ref.at[j], held.at[0, j], s_mate.at[j], r_mate.at[j], mate_id)
        copy.start()
        near.append(copy)
    for j in range(chunks):
        far[j].wait_recv()
        copy = send(held.at[1, j], held.at[2, j], s_fwd.at[j], r_fwd.at[j], mate_id)
        copy.start()
        fwd.append(copy)
    for j in range(chunks):
        near[j].wait_recv()
        fwd[j].wait_recv()
        own = mixed_ref[j]
        near_rows = held[0, j]
        far_rows = held[1, j]
        fwd_rows = held[2, j]
        low_near = jnp.where(core == 0, own, near_rows)
        high_near = jnp.where(core == 0, near_rows, own)
        low_far = jnp.where(core == 0, far_rows, fwd_rows)
        high_far = jnp.where(core == 0, fwd_rows, far_rows)
        upper = me >= 2
        rows = [
            jnp.where(upper, low_far, low_near),
            jnp.where(upper, high_far, high_near),
            jnp.where(upper, low_near, low_far),
            jnp.where(upper, high_near, high_far),
        ]
        total = jnp.zeros(out_ref.shape[1:], jnp.float32)
        for g in range(4):
            total = total + jnp.dot(rows[g], weight_ref[g], preferred_element_type=jnp.float32)
        out_ref[j] = total
    for j in range(chunks):
        far[j].wait_send()
        near[j].wait_send()
        fwd[j].wait_send()


def mix_out(mixed_low, weight_full):
    rows, local_width = mixed_low.shape
    width = weight_full.shape[-1]
    blocks = mixed_low.reshape(CHUNKS, rows // CHUNKS, local_width)
    out = pl.pallas_call(
        mix_kernel,
        out_shape=jax.ShapeDtypeStruct((CHUNKS, rows // CHUNKS, width), jnp.float32),
        in_specs=[VMEM] * 2,
        out_specs=VMEM,
        scratch_shapes=[pltpu.VMEM((3,) + blocks.shape, jnp.bfloat16)]
        + [pltpu.SemaphoreType.DMA((CHUNKS,))] * 6,
        compiler_params=pltpu.CompilerParams(
            collective_id=0, has_side_effects=True, vmem_limit_bytes=48 * 1024 * 1024
        ),
    )(blocks, weight_full)
    return out.reshape(rows, width)


def exchange_kernel(n_sum, n_grad, has_small, dp, *refs):
    refs = list(refs)

    def take(count):
        taken = refs[:count]
        del refs[:count]
        return taken

    sums = take(n_sum)
    grads = take(n_grad)
    small = take(1)[0] if has_small else None
    sum_outs = take(n_sum)
    grad_outs = take(n_grad)
    small_out = take(1)[0] if has_small else None
    from_mate = take(n_sum)
    chip_sum = take(n_sum)
    from_far = take(n_sum)
    pair_in = take(n_grad)
    pair_sum = take(n_grad)
    line_in = take(n_grad)
    small_in = take(1)[0] if has_small else None
    s1, r1, s2, r2, s3, r3, sx, rx, sz, rz = take(10)
    ss, rs, head_in, st, rt = take(5) if has_small else (None,) * 5

    me, core, mate, across = tensor_peers()
    mate_id, far_id = {"tensor": mate}, {"tensor": across}
    here = lax.axis_index("dp")
    side = lax.rem(here, 2)
    line = here // 2
    length = dp // 2
    pair_id = {"dp": here + 1 - 2 * side}
    places = [lax.rem(line + k, length) for k in range(length)]
    line_ids = [{"dp": places[k] * 2 + side} for k in range(length)]
    all_ids = [{"dp": lax.rem(here + k, dp)} for k in range(dp)]
    if has_small:
        group_ids = [{"tensor": lax.rem(me + k, 4)} for k in range(4)]
        greet(group_ids[1:] + all_ids[1:])
    else:
        greet([mate_id, far_id, pair_id] + line_ids[1:])

    started = []
    chunks = CHUNKS
    first = [[None] * chunks for _ in range(n_sum)]
    second = [[None] * chunks for _ in range(n_sum)]
    third = [[None] * chunks for _ in range(n_sum)]
    for i in range(n_sum):
        for j in range(chunks):
            first[i][j] = send(
                sums[i].at[1 - core, j], from_mate[i].at[j], s1.at[i, j], r1.at[i, j], mate_id
            )
            first[i][j].start()
    order = list(range(1, length)) + [0]
    pair = [[None] * length for _ in range(n_grad)]
    for k in order:
        for g in range(n_grad):
            pair[g][k] = send(
                grads[g].at[places[k], 1 - side],
                pair_in[g].at[k],
                sx.at[g, k],
                rx.at[g, k],
                pair_id,
            )
            pair[g][k].start()
    little = []
    if has_small:
        for k in range(1, dp):
            copy = send(small, small_in.at[dp - k], ss.at[k], rs.at[dp - k], all_ids[k])
            copy.start()
            little.append(copy)

    for i in range(n_sum):
        for j in range(chunks):
            first[i][j].wait_recv()
            chip_sum[i][j] = (
                sums[i][core, j].astype(jnp.float32) + from_mate[i][j].astype(jnp.float32)
            ).astype(jnp.bfloat16)
            second[i][j] = send(
                chip_sum[i].at[j], from_far[i].at[j], s2.at[i, j], r2.at[i, j], far_id
            )
            second[i][j].start()

    across_line = [[None] * length for _ in range(n_grad)]
    for k in order:
        for g in range(n_grad):
            pair[g][k].wait_recv()
            pair_sum[g][k] = (
                grads[g][places[k], side].astype(jnp.float32) + pair_in[g][k].astype(jnp.float32)
            ).astype(jnp.bfloat16)
            if k:
                across_line[g][k] = send(
                    pair_sum[g].at[k],
                    line_in[g].at[length - k],
                    sz.at[g, k],
                    rz.at[g, length - k],
                    line_ids[k],
                )
                across_line[g][k].start()

    group = []
    if has_small:
        for copy in little:
            copy.wait_recv()
        small_in[0] = small[...]
        total = small_in[lax.rem(dp - here, dp)]
        for source in range(1, dp):
            total = total + small_in[lax.rem(source + dp - here, dp)]
        small_out[...] = total
        head_in[0] = total[:HEAD_ROWS]
        for k in range(1, 4):
            copy = send(
                head_in.at[0], head_in.at[4 - k], st.at[k], rt.at[4 - k], group_ids[k]
            )
            copy.start()
            group.append(copy)

    for i in range(n_sum):
        for j in range(chunks):
            second[i][j].wait_recv()
            sum_outs[i][core, j] = (
                chip_sum[i][j].astype(jnp.float32) + from_far[i][j].astype(jnp.float32)
            ).astype(jnp.bfloat16)
            third[i][j] = send(
                sum_outs[i].at[core, j],
                sum_outs[i].at[core, j],
                s3.at[i, j],
                r3.at[i, j],
                mate_id,
            )
            third[i][j].start()

    for g in range(n_grad):
        total = pair_sum[g][0].astype(jnp.float32)
        for k in range(1, length):
            across_line[g][length - k].wait_recv()
            total = total + line_in[g][k].astype(jnp.float32)
        grad_outs[g][...] = total
    if has_small:
        for copy in group:
            copy.wait_recv()
        total = head_in[lax.rem(4 - me, 4)]
        for source in range(1, 4):
            total = total + head_in[lax.rem(source + 4 - me, 4)]
        small_out[:HEAD_ROWS] = total
    for i in range(n_sum):
        for j in range(chunks):
            third[i][j].wait_recv()
            first[i][j].wait_send()
            second[i][j].wait_send()
            third[i][j].wait_send()
    for g in range(n_grad):
        for k in range(length):
            pair[g][k].wait_send()
            if k:
                across_line[g][k].wait_send()
    for copy in little + group:
        copy.wait_send()


def exchange(sums, grads, small, dp, collective_id):
    rows, width = sums[0].shape
    chunk_rows = rows // (2 * CHUNKS)
    sum_shape = (2, CHUNKS, chunk_rows, width)
    half_shape = sum_shape[1:]
    sums = [item.astype(jnp.bfloat16).reshape(sum_shape) for item in sums]
    length = dp // 2
    shares = [(item.shape[0] // dp, item.shape[1]) for item in grads]
    grads = [
        item.astype(jnp.bfloat16).reshape((length, 2) + share)
        for item, share in zip(grads, shares)
    ]
    n_sum, n_grad = len(sums), len(grads)
    has_small = small is not None
    operands = sums + grads + ([small] if has_small else [])
    out_shape = [jax.ShapeDtypeStruct(sum_shape, jnp.bfloat16)] * n_sum
    out_shape += [jax.ShapeDtypeStruct(share, jnp.float32) for share in shares]
    if has_small:
        out_shape.append(jax.ShapeDtypeStruct(small.shape, small.dtype))
    scratch = [pltpu.VMEM(half_shape, jnp.bfloat16)] * (3 * n_sum)
    for _ in range(3):
        scratch += [pltpu.VMEM((length,) + share, jnp.bfloat16) for share in shares]
    if has_small:
        scratch.append(pltpu.VMEM((dp,) + small.shape, jnp.float32))
    scratch += [pltpu.SemaphoreType.DMA((n_sum, CHUNKS))] * 6
    scratch += [pltpu.SemaphoreType.DMA((n_grad, length))] * 4
    if has_small:
        scratch += [pltpu.SemaphoreType.DMA((dp,))] * 2
        scratch.append(pltpu.VMEM((4, HEAD_ROWS, small.shape[1]), jnp.float32))
        scratch += [pltpu.SemaphoreType.DMA((4,))] * 2
    outs = pl.pallas_call(
        functools.partial(exchange_kernel, n_sum, n_grad, has_small, dp),
        out_shape=out_shape,
        in_specs=[VMEM] * len(operands),
        out_specs=[VMEM] * len(out_shape),
        scratch_shapes=scratch,
        compiler_params=pltpu.CompilerParams(
            collective_id=collective_id,
            has_side_effects=True,
            vmem_limit_bytes=48 * 1024 * 1024,
        ),
        cost_estimate=pl.CostEstimate(
            flops=10**10, bytes_accessed=6 * 10**7, transcendentals=0
        ),
    )(*operands)
    summed = [item.reshape(rows, width) for item in outs[:n_sum]]
    scattered = list(outs[n_sum : n_sum + n_grad])
    return summed, scattered, (outs[-1] if has_small else None)


def core_halves(rows):
    half = rows.shape[0] // 2
    core = lax.axis_index("tensor") % 2
    return (
        lax.dynamic_slice_in_dim(rows, core * half, half, 0),
        lax.dynamic_slice_in_dim(rows, (1 - core) * half, half, 0),
    )


def to_mate(block):
    return lax.ppermute(block, "tensor", [(i, i ^ 1) for i in range(4)])


def to_far(block):
    return lax.ppermute(block, "tensor", [(i, (i + 2) % 4) for i in range(4)])


def pair_halves(grad, dp):
    side = lax.axis_index("dp") % 2
    low = grad.astype(jnp.bfloat16).reshape(dp // 2, 2, grad.shape[0] // dp, grad.shape[1])
    return (
        lax.dynamic_index_in_dim(low, side, 1, keepdims=False),
        lax.dynamic_index_in_dim(low, 1 - side, 1, keepdims=False),
    )


def to_pair(block, dp):
    return lax.ppermute(block, "dp", [(i, i ^ 1) for i in range(dp)])


def along_line(pair, dp):
    length = dp // 2
    line = lax.axis_index("dp") // 2
    blocks = [lax.dynamic_index_in_dim(pair, line, 0, keepdims=False)]
    for k in range(1, length):
        block = lax.dynamic_index_in_dim(pair, (line + k) % length, 0, keepdims=False)
        ring = [(i, ((i // 2 + k) % length) * 2 + i % 2) for i in range(dp)]
        blocks.append(lax.ppermute(block, "dp", ring))
    return blocks


def add_low(left, right):
    return (left.astype(jnp.float32) + right.astype(jnp.float32)).astype(jnp.bfloat16)


def local(
    tokens,
    segment_ids,
    cotangent,
    first_norm_scale,
    first_norm_bias,
    qkv_weight,
    qkv_bias,
    out_weight,
    out_bias,
    second_norm_scale,
    second_norm_bias,
    fc_weight,
    fc_bias,
    proj_weight,
    proj_bias,
):
    total_rows, model_width = tokens.shape
    dp = lax.axis_size("dp")
    seq_count, seq_length = segment_ids.shape
    local_width = out_weight.shape[0]
    head_dim = model_width // HEADS
    local_heads = local_width // head_dim

    out_weight_full = lax.all_gather(out_weight, "tensor", axis=0)
    residual = tokens.astype(jnp.float32)
    xhat_one, rstd_one = layer_statistics(residual)
    normed_one = (xhat_one * first_norm_scale + first_norm_bias).astype(jnp.bfloat16)
    qkv_low = [
        (
            jnp.dot(normed_one, qkv_weight[:, c], preferred_element_type=jnp.float32)
            + qkv_bias[c]
        )
        .astype(jnp.bfloat16)
        .reshape(seq_count, seq_length, local_heads, head_dim)
        for c in range(3)
    ]
    forward = [
        attend_sequence((qkv_low[0][i], qkv_low[1][i], qkv_low[2][i], segment_ids[i]))
        for i in range(seq_count)
    ]
    mixed_low = (
        jnp.stack([item[0] for item in forward])
        .reshape(total_rows, local_width)
        .astype(jnp.bfloat16)
    )
    middle = residual + mix_out(mixed_low, out_weight_full) + out_bias
    xhat_two, rstd_two = layer_statistics(middle)
    normed_two = (xhat_two * second_norm_scale + second_norm_bias).astype(jnp.bfloat16)
    hidden_pre = jnp.dot(normed_two, fc_weight, preferred_element_type=jnp.float32) + fc_bias
    hidden_act, gelu_pull = jax.vjp(gelu_tanh, hidden_pre)
    hidden_low = hidden_act.astype(jnp.bfloat16)
    out_part = jnp.dot(hidden_low, proj_weight, preferred_element_type=jnp.float32)
    cot = cotangent.astype(jnp.float32)
    proj_bias_grad = jnp.sum(cot, axis=0)
    proj_grad = inner_rows(cotangent, hidden_low)
    act_grad = times_transposed(cotangent, proj_weight)
    pre_grad = gelu_pull(act_grad)[0].astype(jnp.bfloat16)
    fc_bias_grad = jnp.sum(pre_grad.astype(jnp.float32), axis=0)
    fc_grad = inner_rows(normed_two, pre_grad)
    normed_two_part = times_transposed(pre_grad, fc_weight)

    after = lax.optimization_barrier
    own_rows, other_rows = core_halves(out_part.astype(jnp.bfloat16))
    mate_rows = to_mate(other_rows)
    normed_two_part, proj_grad, mate_rows, fc_grad = after(
        (normed_two_part, proj_grad, mate_rows, fc_grad.astype(jnp.bfloat16))
    )
    chip_rows = add_low(own_rows, mate_rows)
    own_fc, other_fc = pair_halves(fc_grad, dp)
    (normed_two_grad,), (proj_sum,), _ = exchange([normed_two_part], [proj_grad], None, dp, 1)
    normed_two_grad, chip_rows, other_fc = after((normed_two_grad, chip_rows, other_fc))
    far_rows = to_far(chip_rows)
    pair_fc = to_pair(other_fc, dp)
    normed_two_grad = normed_two_grad.astype(jnp.float32)
    gain_two_grad = jnp.sum(normed_two_grad * xhat_two, axis=0)
    shift_two_grad = jnp.sum(normed_two_grad, axis=0)
    middle_grad = cot + norm_backward_pass(normed_two_grad, xhat_two, rstd_two, second_norm_scale)
    middle_low = middle_grad.astype(jnp.bfloat16)
    out_bias_grad = jnp.sum(middle_low.astype(jnp.float32), axis=0)
    out_grad = inner_rows(middle_low, mixed_low)
    grad_heads = (
        times_transposed(middle_low, out_weight)
        .astype(jnp.bfloat16)
        .reshape(seq_count, seq_length, local_heads, head_dim)
    )
    middle_kept = core_halves(middle)[0]
    backward = []
    for i in range(seq_count):
        grads, pair_fc = attend_back(
            (
                qkv_low[0][i],
                qkv_low[1][i],
                qkv_low[2][i],
                grad_heads[i],
                forward[i][1],
                segment_ids[i],
            ),
            pair_fc,
        )
        backward.append(grads)
    fc_blocks = along_line(add_low(own_fc, pair_fc), dp)
    qkv_grad = jnp.concatenate(
        [
            jnp.stack([item[c] for item in backward])
            .reshape(total_rows, local_width)
            .astype(jnp.bfloat16)
            for c in range(3)
        ],
        axis=1,
    )
    qkv_grad, fc_blocks, far_rows = after((qkv_grad, fc_blocks, far_rows))
    fc_sum = sum(block.astype(jnp.float32) for block in fc_blocks)
    block_rows = (
        middle_kept + (chip_rows.astype(jnp.float32) + far_rows.astype(jnp.float32)) + proj_bias
    ).astype(jnp.bfloat16)
    rest_rows = to_mate(block_rows)
    qkv_bias_grad = jnp.sum(qkv_grad.astype(jnp.float32), axis=0)
    qkv_weight_grad = inner_rows(normed_one, qkv_grad)
    normed_one_part = times_transposed(
        qkv_grad, qkv_weight.reshape(model_width, 3 * local_width)
    )
    small_parts = [
        jnp.sum(normed_one_part * xhat_one, axis=0),
        jnp.sum(normed_one_part, axis=0),
        gain_two_grad,
        shift_two_grad,
        out_bias_grad,
        proj_bias_grad,
        fc_bias_grad,
        qkv_bias_grad,
    ]
    widest = max(part.shape[0] for part in small_parts)
    small = jnp.stack([jnp.pad(part, (0, widest - part.shape[0])) for part in small_parts])
    normed_one_part, rest_rows, small = after((normed_one_part, rest_rows, small))
    (normed_one_grad,), (qkv_sum, out_sum), small_sum = exchange(
        [normed_one_part], [qkv_weight_grad, out_grad], small, dp, 2
    )
    normed_one_grad = normed_one_grad.astype(jnp.float32)
    tokens_grad = middle_grad + norm_backward_pass(
        normed_one_grad, xhat_one, rstd_one, first_norm_scale
    )
    summed = [small_sum[at, : part.shape[0]] for at, part in enumerate(small_parts)]
    even_core = lax.axis_index("tensor") % 2 == 0
    block_out = jnp.concatenate(
        [jnp.where(even_core, block_rows, rest_rows), jnp.where(even_core, rest_rows, block_rows)]
    )
    share = model_width // dp
    return (
        block_out,
        tokens_grad.astype(jnp.bfloat16),
        summed[0],
        summed[1],
        qkv_sum.reshape(share, 3, local_width),
        summed[7].reshape(3, local_width),
        out_sum.T,
        summed[4],
        summed[2],
        summed[3],
        fc_sum,
        summed[6],
        proj_sum.T,
        summed[5],
    )


def solution(mesh):
    in_specs = (
        P("dp", None),
        P("dp", None),
        P("dp", None),
        P(),
        P(),
        P(None, None, "tensor"),
        P(None, "tensor"),
        P("tensor", None),
        P(),
        P(),
        P(),
        P(None, "tensor"),
        P("tensor"),
        P("tensor", None),
        P(),
    )
    out_specs = (
        P("dp", None),
        P("dp", None),
        P(),
        P(),
        P("dp", None, "tensor"),
        P(None, "tensor"),
        P("tensor", "dp"),
        P(),
        P(),
        P(),
        P("dp", "tensor"),
        P("tensor"),
        P("tensor", "dp"),
        P(),
    )
    return jax.shard_map(local, mesh=mesh, in_specs=in_specs, out_specs=out_specs, check_vma=False)
```
